256 devices in a mesh: pop: 32 (over y_lo, z, core), fsdp: 8 (over y_hi, x).
Axes of the slice: x: 4, y: 4 (y_hi: 2, y_lo: 2; y = y_hi * 2 + y_lo), z: 8, core: 2. Of those that a mesh axis runs over, the one named last changes fastest.
Arguments:
- tokens: bfloat16 [28672, 4096], P('pop', 'fsdp'), may hold values from -6 to 6
- up_weight: bfloat16 [4096, 14336], P('pop', 'fsdp'), may hold values from -0.09375 to 0.09375
- a_bank: bfloat16 [1024, 4096], P(None, 'pop'), may hold values from -6 to 6
- b_bank: bfloat16 [1024, 14336], P(None, 'fsdp'), may hold values from -6 to 6
- factor_index: int32 [64, 4], replicated, may hold values from 0 to 1023
- mirror: int32 [64], P('pop'), may hold values 0 or 1
- rewards: int32 [64], P('pop'), may hold values from -8 to 7
Outputs:
- hidden: bfloat16 [28672, 14336], P('pop', 'fsdp')
- update: float32 [4096, 14336], P('pop', 'fsdp')
The draws below stay inside these ranges and needn't reach their ends.
All inputs are finite; a program needn't handle non-finite values. No bound on the sum of `mirror` on one device may be relied on, other than what follows from the above.
Results may differ from the reference program's by a relative error of at most 0.001.
Values may be sent and summed in bfloat16 or wider, within the bound.
A program may use at most 128 MiB of HBM per device.

```python
import math
import jax
import jax.numpy as jnp
from jax import lax

D = 4096
FF = 14336
RANK = 4
SEQ = 448
BANK = 1024
MEMBERS = 64
TOKENS = 28672


def place_ends(entries, stream_key, smallest, largest):
    dims = entries.shape
    index_at = [jax.random.randint(jax.random.fold_in(stream_key, axis), (), 0, dims[axis]) for axis in range(len(dims))]
    entries = entries.at[tuple(index_at)].set(smallest)
    longest = dims.index(max(dims))
    index_at[longest] = (index_at[longest] + 1) % dims[longest]
    return entries.at[tuple(index_at)].set(largest)


def block_scale(key, extent, split, least, top_value):
    gain = 1.0
    for dim, blocks in split:
        steps = jax.random.uniform(jax.random.fold_in(jax.random.fold_in(key, 6), dim), (blocks,), jnp.float32, least / len(split), top_value / len(split))
        gain = gain * jnp.repeat(jnp.exp(steps), extent[dim] // blocks).reshape((-1,) + (1,) * (len(extent) - 1 - dim))
    return gain


def normal_values(stream_key, extent, deviation, limit, shards=(), held_as=jnp.bfloat16):
    result = jax.random.normal(stream_key, extent, jnp.float32) * deviation
    if len(shards) > 0:
        result = block_scale(stream_key, extent, shards, -0.22, 0.18) * result
    return jnp.clip(result, min=-limit, max=limit).astype(held_as)


def setup_inputs(seed: int = 0) -> dict:
    key_list = jax.random.split(jax.random.key(seed), 8)
    return {
        "tokens": normal_values(key_list[0], (TOKENS, D), 1.0, 6.0, ((0, 32), (1, 8))),
        "up_weight": normal_values(key_list[1], (D, FF), D ** -0.5, 0.09375, ((0, 32), (1, 8))),
        "a_bank": normal_values(key_list[2], (BANK, D), 1.0, 6.0, ((1, 32),)),
        "b_bank": normal_values(key_list[3], (BANK, FF), 1.0, 6.0, ((1, 8),)),
        "factor_index": place_ends(jax.random.randint(key_list[4], (MEMBERS, RANK), 0, BANK), jax.random.fold_in(key_list[4], 1), 0, BANK - 1).astype(jnp.int32),
        "mirror": place_ends((jax.random.randint(key_list[5], (MEMBERS,), 0, 2) < 1).astype(jnp.int32), jax.random.fold_in(key_list[5], 1), 0, 1),
        "rewards": place_ends(jax.random.randint(key_list[6], (MEMBERS,), -8, 8), jax.random.fold_in(key_list[6], 1), -8, 7).astype(jnp.int32),
    }


noise_scale = 0.5

def shaped_weights(rewards, mirror):
    members_all = rewards.shape[0]
    member_ids = jnp.arange(members_all)
    beaten = rewards[None, :] < rewards[:, None]
    level_tie = (rewards[None, :] == rewards[:, None]) & (member_ids[None, :] < member_ids[:, None])
    standing = lax.optimization_barrier(jnp.sum((beaten | level_tie).astype(jnp.int32), axis=1))
    signed = (2 * mirror - 1).astype(jnp.float32)
    shaped = 2.0 * standing.astype(jnp.float32) / (members_all - 1) - 1.0
    return shaped * signed / math.sqrt(members_all * RANK)

def reference(tokens, up_weight, a_bank, b_bank, factor_index, mirror, rewards):
    members_all = factor_index.shape[0]
    factors_a = a_bank[factor_index]
    factors_b = b_bank[factor_index]
    signed = (2 * mirror - 1).astype(jnp.float32)
    scaling = noise_scale / math.sqrt(D * RANK)
    sequences = tokens.reshape(members_all, SEQ, D)

    def one_member(inputs):
        row_block, rows_a, rows_b, sign_one = inputs
        dense_out = jnp.dot(row_block, up_weight, preferred_element_type=jnp.float32)
        projected = jnp.dot(row_block, rows_a.T, preferred_element_type=jnp.float32)
        perturbed = jnp.dot(projected * (scaling * sign_one), rows_b.astype(jnp.float32), precision=lax.Precision.HIGHEST)
        return (dense_out + perturbed).astype(jnp.bfloat16)
    hidden = lax.map(one_member, (sequences, factors_a, factors_b, signed)).reshape(members_all * SEQ, FF)
    weighting = shaped_weights(rewards, mirror)
    spread = jnp.repeat(weighting, RANK)
    flat_a = factors_a.reshape(members_all * RANK, D).astype(jnp.float32)
    flat_b = factors_b.reshape(members_all * RANK, FF).astype(jnp.float32)
    update = jnp.dot(flat_a.T, spread[:, None] * flat_b, precision=lax.Precision.HIGHEST)
    return (hidden, update)
```

```python
import math

import jax
import jax.numpy as jnp
from jax import lax
from jax.experimental import pallas as pl
from jax.experimental.pallas import tpu as pltpu
from jax.sharding import PartitionSpec as P

D = 4096
RANK = 4
SEQ = 448
MEMBERS = 64
BANK = 1024
ROWS = 896
WIDTH = 1792
TILE = 256
TILES = WIDTH // TILE
PIECES = D // TILE
X, Z, CORES = 4, 8, 2
POP, FSDP = 32, 8
FACTORS = MEMBERS * RANK
SLOT = 128
LAST = 6

noise_scale = 0.5
MESH = pl.DeviceIdType.MESH


def picked(values, table):
    return jnp.dot(values.astype(jnp.bfloat16), table, preferred_element_type=jnp.float32)


def flat_rows(index, rows, first, period):
    row = lax.broadcasted_iota(jnp.int32, (rows, MEMBERS), 0)
    factor = first + lax.rem(row, period)
    chosen = lax.broadcasted_iota(jnp.int32, (rows, MEMBERS), 1) == lax.div(factor, RANK)
    whole = index[...]
    high = lax.div(whole, 32)
    low = whole - high * 32
    parts = [
        jnp.dot(
            chosen.astype(jnp.bfloat16),
            part.astype(jnp.float32).astype(jnp.bfloat16),
            preferred_element_type=jnp.float32,
        )
        for part in (high, low)
    ]
    of_member = (parts[0] * 32.0 + parts[1]).astype(jnp.int32)
    row = lax.broadcasted_iota(jnp.int32, (rows, RANK), 0)
    rank = lax.rem(first + lax.rem(row, period), RANK)
    column = lax.broadcasted_iota(jnp.int32, (rows, RANK), 1)
    return jnp.sum(jnp.where(column == rank, of_member, 0), axis=1, keepdims=True)


def one_hot(rows_of, rows):
    return (lax.broadcasted_iota(jnp.int32, (rows, BANK), 1) == rows_of).astype(jnp.float32)


def kernel(
    tokens, weight, a_bank, b_bank, index, mirror, rewards,
    hidden, update,
    tok, wts, acc, out, upd, banka, bankb, pick_a, pick_b, own_b, own_a, message, heard, low,
    w_got, w_sent, t_got, t_sent, m_got, m_sent, local,
):
    p = lax.axis_index("pop")
    f = lax.axis_index("fsdp")
    yl, z, c = p // 16, (p // 2) % Z, p % 2
    yh, x = f // X, f % X

    def pop_of(yl_, z_, c_):
        return yl_ * 16 + lax.rem(z_ + 2 * Z, Z) * 2 + c_

    def fsdp_of(yh_, x_):
        return yh_ * X + lax.rem(x_ + 2 * X, X)

    def sibling():
        return {"pop": pop_of(yl, z, 1 - c), "fsdp": f}

    def along_z(way):
        return {"pop": pop_of(yl, z + way, c), "fsdp": f}

    def across_y():
        return {"pop": pop_of(1 - yl, z, c), "fsdp": f}

    def along_x(way):
        return {"pop": p, "fsdp": fsdp_of(yh, x + way)}

    def far_y():
        return {"pop": p, "fsdp": fsdp_of(1 - yh, x)}

    barrier = pltpu.get_barrier_semaphore()

    def greet(j, _):
        peer = lax.rem(p + j, POP)
        pl.semaphore_signal(barrier, inc=1, device_id={"pop": peer, "fsdp": f}, device_id_type=MESH)
        return 0

    for way in (1, -1):
        pl.semaphore_signal(barrier, inc=1, device_id=along_x(way), device_id_type=MESH)
    pl.semaphore_signal(barrier, inc=1, device_id=far_y(), device_id_type=MESH)
    lax.fori_loop(1, POP, greet, 0)

    load_a = pltpu.make_async_copy(a_bank, banka, local.at[0])
    load_b = pltpu.make_async_copy(b_bank, bankb, local.at[1])
    load_t = pltpu.make_async_copy(tokens, tok.at[f], local.at[2])
    load_w = pltpu.make_async_copy(
        weight, wts.at[pl.ds(pl.multiple_of(p * 128, 128), 128)], local.at[3]
    )
    for copy in (load_a, load_w, load_t, load_b):
        copy.start()
    pl.semaphore_wait(barrier, POP - 1 + 3)

    sends = []

    def w_block(shard, half):
        return wts.at[pl.ds(pl.multiple_of(shard * 128 + half * 64, 64), 64)]

    def t_block(owner, half):
        return tok.at[owner, pl.ds(half * SEQ, SEQ)]

    counts = {"w": 0, "t": 0}

    def send_w(shard, half, target, own=False):
        k = counts["w"]
        counts["w"] += 1
        copy = pltpu.make_async_remote_copy(
            src_ref=weight.at[pl.ds(half * 64, 64)] if own else w_block(shard, half),
            dst_ref=w_block(shard, half),
            send_sem=w_sent.at[k],
            recv_sem=w_got.at[shard * 2 + half],
            device_id=target,
            device_id_type=MESH,
        )
        copy.start()
        sends.append(copy)

    def send_t(owner, half, target, own=False):
        k = counts["t"]
        counts["t"] += 1
        copy = pltpu.make_async_remote_copy(
            src_ref=tokens.at[pl.ds(half * SEQ, SEQ)] if own else t_block(owner, half),
            dst_ref=t_block(owner, half),
            send_sem=t_sent.at[k],
            recv_sem=t_got.at[owner * 2 + half],
            device_id=target,
            device_id_type=MESH,
        )
        copy.start()
        sends.append(copy)

    def wait_w(shard, half):
        block = w_block(shard, half)
        pltpu.make_async_copy(block, block, w_got.at[shard * 2 + half]).wait()

    def wait_t(owner, half):
        block = t_block(owner, half)
        pltpu.make_async_copy(block, block, t_got.at[owner * 2 + half]).wait()

    for half in (0, 1):
        for way in (1, -1):
            send_w(p, half, along_z(way), True)
        send_w(p, half, across_y(), True)
        for way in (1, -1):
            send_t(f, half, along_x(way), True)
        send_t(f, half, far_y(), True)
        send_w(p, half, sibling(), True)

    owed = [(pop_of(yl, z, 1 - c), 0), (pop_of(yl, z, 1 - c), 1)]

    def settle():
        for shard, half in owed:
            wait_w(shard, half)
        owed.clear()

    def got_own(d, way, half):
        z_ = z - way * d
        shard = pop_of(yl, z_, c)
        wait_w(shard, half)
        if d < 3 or (d == 3 and half == (0 if way == 1 else 1)):
            send_w(shard, half, along_z(way))
        send_w(shard, half, sibling())
        if (d == 3 and half == 1) or d == 4:
            send_w(shard, half, across_y())
        owed.append((pop_of(yl, z_, 1 - c), half))

    def got_other(d, way, half, forward=True):
        z_ = z - way * d
        shard = pop_of(1 - yl, z_, c)
        wait_w(shard, half)
        if forward and (d == 1 or (d == 2 and half == 0)):
            send_w(shard, half, along_z(way))
        send_w(shard, half, sibling())
        owed.append((pop_of(1 - yl, z_, 1 - c), half))

    def pass_other(half):
        for way in (1, -1):
            send_w(pop_of(1 - yl, z, c), half, along_z(way))

    def got_tokens(yh_, d, way, half):
        owner = fsdp_of(yh_, x - way * d)
        wait_t(owner, half)
        if d == 1 and half == (0 if way == 1 else 1):
            send_t(owner, half, along_x(way))

    def pass_tokens(half):
        for way in (1, -1):
            send_t(fsdp_of(1 - yh, x), half, along_x(way))

    load_a.wait()
    hot = one_hot(flat_rows(index, FACTORS, 0, FACTORS), FACTORS).astype(jnp.bfloat16)
    rows_a = picked(hot, banka[...])
    pick_a[...] = rows_a
    line = lax.broadcasted_iota(jnp.int32, (8, 128), 0)
    info = jnp.where(
        line == 0,
        rewards[0].astype(jnp.float32),
        jnp.where(
            line == 1,
            rewards[1].astype(jnp.float32),
            jnp.where(line == 2, mirror[0].astype(jnp.float32), mirror[1].astype(jnp.float32)),
        ),
    )
    message[...] = jnp.concatenate(
        [rows_a.reshape(POP, 8, 128), jnp.broadcast_to(info[None], (POP, 8, 128))], axis=1
    ).astype(jnp.bfloat16)

    def tell(j, _):
        peer = lax.rem(p + j, POP)
        pltpu.make_async_remote_copy(
            src_ref=message.at[peer],
            dst_ref=heard.at[p],
            send_sem=m_sent.at[j],
            recv_sem=m_got.at[p],
            device_id={"pop": peer, "fsdp": f},
            device_id_type=MESH,
        ).start()
        return 0

    lax.fori_loop(1, POP, tell, 0)
    heard[p] = message[p]

    for way in (1, -1):
        got_own(1, way, 0)

    load_b.wait()
    pick_b[...] = picked(hot, bankb[...]).astype(jnp.bfloat16)
    hot_own = one_hot(flat_rows(index, SLOT, p * 8, 8), SLOT)
    used = lax.broadcasted_iota(jnp.int32, (SLOT, BANK), 0) < 24
    own_b[...] = picked(jnp.where(used, hot_own, 0.0), bankb[...]).astype(jnp.bfloat16)
    acc[...] = jnp.zeros_like(acc)
    low[...] = jnp.zeros_like(low)

    for way in (1, -1):
        got_own(1, way, 1)

    def hear(j, _):
        peer = lax.rem(p + POP - j, POP)
        block = heard.at[peer]
        pltpu.make_async_copy(block, block, m_got.at[peer]).wait()
        return 0

    lax.fori_loop(1, POP, hear, 0)

    def lay(q, _):
        both = jnp.concatenate([heard[2 * q], heard[2 * q + 1]], axis=1).astype(jnp.float32)[:8]
        own_a[q] = jnp.concatenate(
            [both, both, both, jnp.zeros((SLOT - 24, TILE), jnp.float32)], axis=0
        ).astype(jnp.bfloat16)
        return 0

    lax.fori_loop(0, PIECES, lay, 0)

    told = heard[...].astype(jnp.float32)[:, 8:16, :].reshape(POP * 8, 128)
    row = lax.broadcasted_iota(jnp.int32, (FACTORS, POP * 8), 0)
    place = lax.broadcasted_iota(jnp.int32, (FACTORS, POP * 8), 1)
    member = lax.div(row, RANK)
    spot = lax.div(member, 2) * 8 + lax.rem(member, 2)
    told16 = told.astype(jnp.bfloat16)
    reward_of = picked((place == spot).astype(jnp.float32), told16)
    mirror_of = picked((place == spot + 2).astype(jnp.float32), told16)
    lane = lax.broadcasted_iota(jnp.int32, (POP * 8, 128), 1)
    at = lax.broadcasted_iota(jnp.int32, (POP * 8, 128), 0)
    mine = at == lax.div(lane, 2) * 8 + lax.rem(lane, 2)
    across = jnp.sum(jnp.where(mine, told, 0.0), axis=0, keepdims=True)
    lane = lax.broadcasted_iota(jnp.int32, (FACTORS, 128), 1)
    member = lax.div(lax.broadcasted_iota(jnp.int32, (FACTORS, 128), 0), RANK)
    ahead = (across < reward_of) | ((across == reward_of) & (lane < member))
    standing = jnp.sum(
        jnp.where(ahead & (lane < MEMBERS), 1.0, 0.0), axis=1, keepdims=True
    )
    coeff = (2.0 * standing - (MEMBERS - 1)) * (2.0 * mirror_of - 1.0)
    shaped = pick_a[...] * coeff
    high = shaped.astype(jnp.bfloat16)
    rest = (shaped - high.astype(jnp.float32)).astype(jnp.bfloat16)
    both = jnp.concatenate([high, rest], axis=0).astype(jnp.float32).T.astype(jnp.bfloat16)
    rows_b = pick_b[...]
    total = jnp.dot(
        both, jnp.concatenate([rows_b, rows_b], axis=0), preferred_element_type=jnp.float32
    )
    upd[...] = total * (1.0 / ((MEMBERS - 1) * math.sqrt(MEMBERS * RANK)))
    save_u = pltpu.make_async_copy(upd, update, local.at[4])
    save_u.start()

    def phase_of(q):
        x_, yl_, z_ = lax.rem(lax.div(q, 2), X), lax.div(q, Z), lax.rem(q, Z)
        dx = lax.rem(x_ - x + X, X)
        dz = lax.rem(z_ - z + Z, Z)
        dz = jnp.minimum(dz, Z - dz)
        near = jnp.where(dx == 2, 2, 1)
        far = jnp.where(dx == 0, 2, jnp.where(dx == 2, 6, 4))
        by_tokens = jnp.where(yl_ == yh, near, far)
        same = jnp.where(dz < 3, 1, 2)
        other = jnp.where(
            dz == 0, 1, jnp.where(dz == 1, 3, jnp.where(dz == 2, 5, jnp.where(dz == 3, 6, 4)))
        )
        by_weight = jnp.where(yl_ == yl, same, other)
        return jnp.maximum(by_tokens, by_weight)

    def work(q):
        lhs = tok[lax.div(q, 2), :, pl.ds(pl.multiple_of(lax.rem(q, 2) * TILE, TILE), TILE)]

        def tile(n, _):
            rhs = wts[
                pl.ds(pl.multiple_of(q * TILE, TILE), TILE),
                pl.ds(pl.multiple_of(n * TILE, TILE), TILE),
            ]
            acc[n] += jnp.dot(lhs, rhs, preferred_element_type=jnp.float32)
            return 0

        lax.fori_loop(0, TILES, tile, 0)
        low[...] += lax.dot_general(
            lhs, own_a[q], (((1,), (1,)), ((), ())), preferred_element_type=jnp.float32
        )

    def phase(number):
        settle()

        def step(q, _):
            @pl.when(phase_of(q) == number)
            def _():
                work(q)

            return 0

        lax.fori_loop(0, PIECES, step, 0)

    for way in (1, -1):
        got_own(2, way, 0)
    for way in (1, -1):
        got_tokens(yh, 1, way, 0)
    got_other(0, 1, 0)
    wait_t(fsdp_of(1 - yh, x), 0)
    pass_tokens(0)
    for way in (1, -1):
        got_own(2, way, 1)
    for way in (1, -1):
        got_tokens(yh, 1, way, 1)
    got_other(0, 1, 1)
    load_t.wait()
    load_w.wait()
    phase(1)
    for way in (1, -1):
        got_own(3, way, 0)
    pass_other(0)
    wait_t(fsdp_of(1 - yh, x), 1)
    pass_tokens(1)
    for way in (1, -1):
        got_own(3, way, 1)
    pass_other(1)
    got_tokens(yh, 2, 1, 0)
    got_tokens(yh, 2, -1, 1)
    got_own(4, 1, 0)
    got_own(4, -1, 1)
    phase(2)
    for half in (0, 1):
        for way in (1, -1):
            got_other(1, way, half)
    for way in (1, -1):
        got_other(3, way, 1, False)
    for way in (1, -1):
        got_tokens(1 - yh, 1, way, 0)
    phase(3)
    for way in (1, -1):
        got_other(2, way, 0)
    got_other(4, 1, 0)
    got_other(4, -1, 1)
    for way in (1, -1):
        got_tokens(1 - yh, 1, way, 1)
    phase(4)
    for way in (1, -1):
        got_other(2, way, 1)
    phase(5)
    for way in (1, -1):
        got_other(3, way, 0, False)
    got_tokens(1 - yh, 2, 1, 0)
    got_tokens(1 - yh, 2, -1, 1)
    phase(LAST)

    lane = lax.broadcasted_iota(jnp.int32, (ROWS, SLOT), 1)
    row = lax.broadcasted_iota(jnp.int32, (ROWS, SLOT), 0)
    own = lax.div(lax.rem(lane, 8), RANK) == lax.div(row, SEQ)
    signed = jnp.where(
        row < SEQ,
        (2 * mirror[0] - 1).astype(jnp.float32),
        (2 * mirror[1] - 1).astype(jnp.float32),
    )
    scaled = jnp.where(own, low[...] * (signed * (noise_scale / math.sqrt(D * RANK))), 0.0)
    first = scaled.astype(jnp.bfloat16).astype(jnp.float32)
    second = (scaled - first).astype(jnp.bfloat16).astype(jnp.float32)
    third = scaled - first - second
    parts = jnp.where(lane < 8, first, jnp.where(lane < 16, second, third)).astype(jnp.bfloat16)

    for n in range(TILES):
        columns = pl.ds(n * TILE, TILE)
        out[:, columns] = (
            acc[n] + jnp.dot(parts, own_b[:, columns], preferred_element_type=jnp.float32)
        ).astype(jnp.bfloat16)
        pltpu.make_async_copy(out.at[:, columns], hidden.at[:, columns], local.at[5 + n]).start()

    for copy in sends:
        copy.wait_send()

    def told_all(j, _):
        peer = lax.rem(p + j, POP)
        pltpu.make_async_copy(message.at[peer], message.at[peer], m_sent.at[j]).wait()
        return 0

    lax.fori_loop(1, POP, told_all, 0)
    save_u.wait()
    for n in range(TILES):
        columns = pl.ds(n * TILE, TILE)
        pltpu.make_async_copy(out.at[:, columns], hidden.at[:, columns], local.at[5 + n]).wait()


def per_device(tokens, up_weight, a_bank, b_bank, factor_index, mirror, rewards):
    any_space = pl.BlockSpec(memory_space=pl.ANY)
    smem = pl.BlockSpec(memory_space=pltpu.SMEM)
    dma = pltpu.SemaphoreType.DMA
    bf16, f32 = jnp.bfloat16, jnp.float32
    return pl.pallas_call(
        kernel,
        out_shape=(
            jax.ShapeDtypeStruct((ROWS, WIDTH), bf16),
            jax.ShapeDtypeStruct((128, WIDTH), f32),
        ),
        in_specs=[any_space] * 4 + [pl.BlockSpec(memory_space=pltpu.VMEM), smem, smem],
        out_specs=(any_space, any_space),
        scratch_shapes=[
            pltpu.VMEM((FSDP, ROWS, 512), bf16),
            pltpu.VMEM((D, WIDTH), bf16),
            pltpu.VMEM((TILES, ROWS, TILE), f32),
            pltpu.VMEM((ROWS, WIDTH), bf16),
            pltpu.VMEM((128, WIDTH), f32),
            pltpu.VMEM((BANK, 128), bf16),
            pltpu.VMEM((BANK, WIDTH), bf16),
            pltpu.VMEM((FACTORS, 128), f32),
            pltpu.VMEM((FACTORS, WIDTH), bf16),
            pltpu.VMEM((SLOT, WIDTH), bf16),
            pltpu.VMEM((PIECES, SLOT, TILE), bf16),
            pltpu.VMEM((POP, 16, 128), bf16),
            pltpu.VMEM((POP, 16, 128), bf16),
            pltpu.VMEM((ROWS, SLOT), f32),
            dma((64,)),
            dma((62,)),
            dma((16,)),
            dma((14,)),
            dma((POP,)),
            dma((POP,)),
            dma((5 + TILES,)),
        ],
        compiler_params=pltpu.CompilerParams(
            collective_id=1, has_side_effects=True, vmem_limit_bytes=56 * 2**20
        ),
        name="gather_project",
    )(tokens, up_weight, a_bank, b_bank, factor_index, mirror, rewards)


def solution(mesh):
    in_specs = (
        P("pop", "fsdp"),
        P("pop", "fsdp"),
        P(None, "pop"),
        P(None, "fsdp"),
        P(),
        P("pop"),
        P("pop"),
    )
    out_specs = (P("pop", "fsdp"), P("pop", "fsdp"))
    return jax.shard_map(
        per_device, mesh=mesh, in_specs=in_specs, out_specs=out_specs, check_vma=False
    )
```

```python
import math

import jax
import jax.numpy as jnp
from jax import lax
from jax.experimental import pallas as pl
from jax.experimental.pallas import tpu as pltpu
from jax.sharding import PartitionSpec as P

D = 4096
RANK = 4
SEQ = 448
MEMBERS = 64
BANK = 1024
ROWS = 896
WIDTH = 1792
TILE = 256
TILES = WIDTH // TILE
PIECES = D // TILE
X, Z, CORES = 4, 8, 2
POP, FSDP = 32, 8
FACTORS = MEMBERS * RANK
SLOT = 128
LAST = 6

noise_scale = 0.5
MESH = pl.DeviceIdType.MESH


def picked(values, table):
    return jnp.dot(values.astype(jnp.bfloat16), table, preferred_element_type=jnp.float32)


def flat_rows(index, rows, first, period):
    row = lax.broadcasted_iota(jnp.int32, (rows, MEMBERS), 0)
    factor = first + lax.rem(row, period)
    chosen = lax.broadcasted_iota(jnp.int32, (rows, MEMBERS), 1) == lax.div(factor, RANK)
    whole = index[...]
    high = lax.div(whole, 32)
    low = whole - high * 32
    parts = [
        lax.dot_general(
            chosen.astype(jnp.bfloat16),
            part.astype(jnp.float32).astype(jnp.bfloat16),
            (((1,), (1,)), ((), ())),
            preferred_element_type=jnp.float32,
        )
        for part in (high, low)
    ]
    of_member = (parts[0] * 32.0 + parts[1]).astype(jnp.int32)
    row = lax.broadcasted_iota(jnp.int32, (rows, RANK), 0)
    rank = lax.rem(first + lax.rem(row, period), RANK)
    column = lax.broadcasted_iota(jnp.int32, (rows, RANK), 1)
    return jnp.sum(jnp.where(column == rank, of_member, 0), axis=1, keepdims=True)


def one_hot(rows_of, rows):
    return (lax.broadcasted_iota(jnp.int32, (rows, BANK), 1) == rows_of).astype(jnp.float32)


def kernel(
    tokens, weight, a_bank, b_bank, index, mirror, rewards,
    hidden, update,
    tok, wts, acc, banka, bankb, pick_a, pick_b, own_b, own_a, message, heard, low,
    w_got, w_sent, t_got, t_sent, m_got, m_sent, local,
):
    p = lax.axis_index("pop")
    f = lax.axis_index("fsdp")
    yl, z, c = p // 16, (p // 2) % Z, p % 2
    yh, x = f // X, f % X

    def pop_of(yl_, z_, c_):
        return yl_ * 16 + lax.rem(z_ + 2 * Z, Z) * 2 + c_

    def fsdp_of(yh_, x_):
        return yh_ * X + lax.rem(x_ + 2 * X, X)

    def sibling():
        return {"pop": pop_of(yl, z, 1 - c), "fsdp": f}

    def along_z(way):
        return {"pop": pop_of(yl, z + way, c), "fsdp": f}

    def across_y():
        return {"pop": pop_of(1 - yl, z, c), "fsdp": f}

    def along_x(way):
        return {"pop": p, "fsdp": fsdp_of(yh, x + way)}

    def far_y():
        return {"pop": p, "fsdp": fsdp_of(1 - yh, x)}

    barrier = pltpu.get_barrier_semaphore()

    def greet(j, _):
        peer = lax.rem(p + j, POP)
        pl.semaphore_signal(barrier, inc=1, device_id={"pop": peer, "fsdp": f}, device_id_type=MESH)
        return 0

    for way in (1, -1):
        pl.semaphore_signal(barrier, inc=1, device_id=along_x(way), device_id_type=MESH)
    pl.semaphore_signal(barrier, inc=1, device_id=far_y(), device_id_type=MESH)
    lax.fori_loop(1, POP, greet, 0)

    load_a = pltpu.make_async_copy(a_bank, banka, local.at[0])
    load_b = pltpu.make_async_copy(b_bank, bankb, local.at[1])
    load_t = pltpu.make_async_copy(tokens, tok.at[f], local.at[2])
    load_w = pltpu.make_async_copy(
        weight, wts.at[pl.ds(pl.multiple_of(p * 128, 128), 128)], local.at[3]
    )
    for copy in (load_a, load_w, load_t, load_b):
        copy.start()

    load_a.wait()
    hot = one_hot(flat_rows(index, FACTORS, 0, FACTORS), FACTORS).astype(jnp.bfloat16)
    rows_a = picked(hot, banka[...])
    pick_a[...] = rows_a
    line = lax.broadcasted_iota(jnp.int32, (8, 128), 0)
    info = jnp.where(
        line == 0,
        rewards[0].astype(jnp.float32),
        jnp.where(
            line == 1,
            rewards[1].astype(jnp.float32),
            jnp.where(line == 2, mirror[0].astype(jnp.float32), mirror[1].astype(jnp.float32)),
        ),
    )
    message[...] = jnp.concatenate(
        [rows_a.reshape(POP, 8, 128), jnp.broadcast_to(info[None], (POP, 8, 128))], axis=1
    ).astype(jnp.bfloat16)

    heard[p] = message[p]
    pl.semaphore_wait(barrier, POP - 1 + 3)

    sends = []

    def w_block(shard, half):
        return wts.at[pl.ds(pl.multiple_of(shard * 128 + half * 64, 64), 64)]

    def t_block(owner, half):
        return tok.at[owner, pl.ds(half * SEQ, SEQ)]

    counts = {"w": 0, "t": 0}

    def send_w(shard, half, target, own=False):
        k = counts["w"]
        counts["w"] += 1
        copy = pltpu.make_async_remote_copy(
            src_ref=weight.at[pl.ds(half * 64, 64)] if own else w_block(shard, half),
            dst_ref=w_block(shard, half),
            send_sem=w_sent.at[k],
            recv_sem=w_got.at[shard * 2 + half],
            device_id=target,
            device_id_type=MESH,
        )
        copy.start()
        sends.append(copy)

    def send_t(owner, half, target, own=False):
        k = counts["t"]
        counts["t"] += 1
        copy = pltpu.make_async_remote_copy(
            src_ref=tokens.at[pl.ds(half * SEQ, SEQ)] if own else t_block(owner, half),
            dst_ref=t_block(owner, half),
            send_sem=t_sent.at[k],
            recv_sem=t_got.at[owner * 2 + half],
            device_id=target,
            device_id_type=MESH,
        )
        copy.start()
        sends.append(copy)

    def wait_w(shard, half):
        block = w_block(shard, half)
        pltpu.make_async_copy(block, block, w_got.at[shard * 2 + half]).wait()

    def wait_t(owner, half):
        block = t_block(owner, half)
        pltpu.make_async_copy(block, block, t_got.at[owner * 2 + half]).wait()

    for turn in (0, 1):
        for way in (1, -1):
            send_w(p, turn if way == 1 else 1 - turn, along_z(way), True)
        for way in (1, -1):
            send_t(f, turn if way == 1 else 1 - turn, along_x(way), True)
        if turn == 0:
            def tell(j, _):
                peer = lax.rem(p + j, POP)
                pltpu.make_async_remote_copy(
                    src_ref=message.at[peer],
                    dst_ref=heard.at[p],
                    send_sem=m_sent.at[j],
                    recv_sem=m_got.at[p],
                    device_id={"pop": peer, "fsdp": f},
                    device_id_type=MESH,
                ).start()
                return 0

            lax.fori_loop(1, POP, tell, 0)
        send_t(f, turn, far_y(), True)
        send_w(p, turn, across_y(), True)
        send_w(p, turn, sibling(), True)

    def phase_of(q):
        x_, yl_, z_ = (q // 2) % X, q // Z, q % Z
        dx = lax.rem(x_ - x + X, X)
        dz = lax.rem(z_ - z + Z, Z)
        dz = jnp.minimum(dz, Z - dz)
        near = jnp.where(dx == 2, 2, 1)
        far = jnp.where(dx == 0, 2, jnp.where(dx == 2, 6, 4))
        by_tokens = jnp.where(yl_ == yh, near, far)
        same = jnp.where(dz < 3, 1, 2)
        other = jnp.where(
            dz == 0, 1, jnp.where(dz == 1, 3, jnp.where(dz == 2, 5, jnp.where(dz == 3, 6, 4)))
        )
        by_weight = jnp.where(yl_ == yl, same, other)
        return jnp.maximum(by_tokens, by_weight)


    keys = [phase_of(q) * PIECES + q for q in range(PIECES)]
    places = [sum((other < key).astype(jnp.int32) for other in keys if other is not key) for key in keys]
    ends = [
        sum((key < (number + 1) * PIECES).astype(jnp.int32) for key in keys)
        for number in range(LAST + 1)
    ]

    def piece_at(k):
        return sum(jnp.where(place == k, q, 0) for q, place in enumerate(places))

    owed = [(pop_of(yl, z, 1 - c), 0), (pop_of(yl, z, 1 - c), 1)]

    def settle():
        for shard, half in owed:
            wait_w(shard, half)
        owed.clear()

    def got_own(d, way, half):
        z_ = z - way * d
        shard = pop_of(yl, z_, c)
        wait_w(shard, half)
        if d < 3 or (d == 3 and half == (0 if way == 1 else 1)):
            send_w(shard, half, along_z(way))
        send_w(shard, half, sibling())
        if (d == 3 and half == 1) or d == 4:
            send_w(shard, half, across_y())
        owed.append((pop_of(yl, z_, 1 - c), half))

    def got_other(d, way, half, forward=True):
        z_ = z - way * d
        shard = pop_of(1 - yl, z_, c)
        wait_w(shard, half)
        if forward and (d == 1 or (d == 2 and half == 0)):
            send_w(shard, half, along_z(way))
        send_w(shard, half, sibling())
        owed.append((pop_of(1 - yl, z_, 1 - c), half))

    def pass_other(half):
        for way in (1, -1):
            send_w(pop_of(1 - yl, z, c), half, along_z(way))

    def got_tokens(yh_, d, way, half):
        owner = fsdp_of(yh_, x - way * d)
        wait_t(owner, half)
        if d == 1 and half == (0 if way == 1 else 1):
            send_t(owner, half, along_x(way))

    def pass_tokens(turn):
        for way in (1, -1):
            send_t(fsdp_of(1 - yh, x), turn if way == 1 else 1 - turn, along_x(way))

    def work(q):
        lhs = tok[lax.div(q, 2), :, pl.ds(pl.multiple_of(lax.rem(q, 2) * TILE, TILE), TILE)]
        features = pl.ds(pl.multiple_of(q * TILE, TILE), TILE)
        for n in range(TILES):
            acc[n] += jnp.dot(
                lhs, wts[features, n * TILE : (n + 1) * TILE], preferred_element_type=jnp.float32
            )
        low[...] += jnp.dot(lhs, own_a[q], preferred_element_type=jnp.float32)

    done = [0]

    def multiply(number, most):
        stop = jnp.minimum(done[0] + most, ends[number])

        def step(k, _):
            work(piece_at(k))
            return 0

        lax.fori_loop(done[0], stop, step, 0)
        done[0] = stop

    def own_turn(d, turn):
        for way in (1, -1):
            got_own(d, way, turn if way == 1 else 1 - turn)

    def other_turn(d, half, forward=True):
        for way in (1, -1):
            got_other(d, way, half, forward)

    def token_turn(yh_, turn):
        for way in (1, -1):
            got_tokens(yh_, 1, way, turn if way == 1 else 1 - turn)

    own_turn(1, 0)
    load_b.wait()
    pick_b[...] = picked(hot, bankb[...]).astype(jnp.bfloat16)
    own_turn(1, 1)
    token_turn(yh, 0)
    hot_own = one_hot(flat_rows(index, SLOT, p * 8, 8), SLOT)
    used = lax.broadcasted_iota(jnp.int32, (SLOT, BANK), 0) < 24
    own_b[...] = picked(jnp.where(used, hot_own, 0.0), bankb[...]).astype(jnp.bfloat16)
    own_turn(2, 0)
    acc[...] = jnp.zeros_like(acc)
    low[...] = jnp.zeros_like(low)
    load_t.wait()
    load_w.wait()
    own_turn(2, 1)
    token_turn(yh, 1)

    def hear(j, _):
        peer = lax.rem(p + POP - j, POP)
        block = heard.at[peer]
        pltpu.make_async_copy(block, block, m_got.at[peer]).wait()
        return 0

    lax.fori_loop(1, POP, hear, 0)

    def lay(q, _):
        both = jnp.concatenate([heard[2 * q], heard[2 * q + 1]], axis=1).astype(jnp.float32)[:8]
        own_a[q] = jnp.concatenate(
            [both, both, both, jnp.zeros((SLOT - 24, TILE), jnp.float32)], axis=0
        ).T.astype(jnp.bfloat16)
        return 0

    lax.fori_loop(0, PIECES, lay, 0)

    for half in (0, 1):
        got_other(0, 1, half)
    own_turn(3, 0)
    settle()
    multiply(1, 2)
    wait_t(fsdp_of(1 - yh, x), 0)
    wait_t(fsdp_of(1 - yh, x), 1)
    for turn in (0, 1):
        pass_tokens(turn)
    own_turn(3, 1)
    pass_other(0)
    pass_other(1)
    got_tokens(yh, 2, 1, 0)
    got_tokens(yh, 2, -1, 1)
    multiply(1, 3)
    got_own(4, 1, 0)
    got_own(4, -1, 1)
    told = heard[...].astype(jnp.float32)[:, 8:16, :].reshape(POP * 8, 128)
    row = lax.broadcasted_iota(jnp.int32, (FACTORS, POP * 8), 0)
    place = lax.broadcasted_iota(jnp.int32, (FACTORS, POP * 8), 1)
    member = lax.div(row, RANK)
    spot = lax.div(member, 2) * 8 + lax.rem(member, 2)
    told16 = told.astype(jnp.bfloat16)
    reward_of = picked((place == spot).astype(jnp.float32), told16)
    mirror_of = picked((place == spot + 2).astype(jnp.float32), told16)
    lane = lax.broadcasted_iota(jnp.int32, (POP * 8, 128), 1)
    at = lax.broadcasted_iota(jnp.int32, (POP * 8, 128), 0)
    mine = at == lax.div(lane, 2) * 8 + lax.rem(lane, 2)
    across = jnp.sum(jnp.where(mine, told, 0.0), axis=0, keepdims=True)
    lane = lax.broadcasted_iota(jnp.int32, (FACTORS, 128), 1)
    member = lax.div(lax.broadcasted_iota(jnp.int32, (FACTORS, 128), 0), RANK)
    ahead = (across < reward_of) | ((across == reward_of) & (lane < member))
    standing = jnp.sum(
        jnp.where(ahead & (lane < MEMBERS), 1.0, 0.0), axis=1, keepdims=True
    )
    coeff = (2.0 * standing - (MEMBERS - 1)) * (2.0 * mirror_of - 1.0)
    shaped = pick_a[...] * coeff
    high = shaped.astype(jnp.bfloat16)
    rest = (shaped - high.astype(jnp.float32)).astype(jnp.bfloat16)
    both = jnp.concatenate([high, rest], axis=0).astype(jnp.float32).T.astype(jnp.bfloat16)
    rows_b = pick_b[...]
    total = jnp.dot(
        both, jnp.concatenate([rows_b, rows_b], axis=0), preferred_element_type=jnp.float32
    )
    update[...] = total * (1.0 / ((MEMBERS - 1) * math.sqrt(MEMBERS * RANK)))

    settle()
    multiply(2, 2)
    other_turn(1, 0)
    token_turn(1 - yh, 0)
    multiply(2, 3)
    other_turn(1, 1)
    other_turn(3, 1, False)
    settle()
    multiply(3, 3)
    other_turn(2, 0)
    got_other(4, 1, 0)
    got_other(4, -1, 1)
    token_turn(1 - yh, 1)
    settle()
    multiply(4, 3)
    other_turn(2, 1)
    settle()
    multiply(5, PIECES)
    other_turn(3, 0, False)
    settle()
    got_tokens(1 - yh, 2, 1, 0)
    got_tokens(1 - yh, 2, -1, 1)
    multiply(LAST, PIECES)

    lane = lax.broadcasted_iota(jnp.int32, (ROWS, SLOT), 1)
    row = lax.broadcasted_iota(jnp.int32, (ROWS, SLOT), 0)
    own = lax.div(lax.rem(lane, 8), RANK) == lax.div(row, SEQ)
    signed = jnp.where(
        row < SEQ,
        (2 * mirror[0] - 1).astype(jnp.float32),
        (2 * mirror[1] - 1).astype(jnp.float32),
    )
    scaled = jnp.where(own, low[...] * (signed * (noise_scale / math.sqrt(D * RANK))), 0.0)
    first = scaled.astype(jnp.bfloat16).astype(jnp.float32)
    second = (scaled - first).astype(jnp.bfloat16).astype(jnp.float32)
    third = scaled - first - second
    parts = jnp.where(lane < 8, first, jnp.where(lane < 16, second, third)).astype(jnp.bfloat16)

    for n in range(TILES):
        columns = pl.ds(n * TILE, TILE)
        hidden[:, columns] = (
            acc[n] + jnp.dot(parts, own_b[:, columns], preferred_element_type=jnp.float32)
        ).astype(jnp.bfloat16)

    for copy in sends:
        copy.wait_send()

    def told_all(j, _):
        peer = lax.rem(p + j, POP)
        pltpu.make_async_copy(message.at[peer], message.at[peer], m_sent.at[j]).wait()
        return 0

    lax.fori_loop(1, POP, told_all, 0)


def per_device(tokens, up_weight, a_bank, b_bank, factor_index, mirror, rewards):
    any_space = pl.BlockSpec(memory_space=pl.ANY)
    smem = pl.BlockSpec(memory_space=pltpu.SMEM)
    dma = pltpu.SemaphoreType.DMA
    bf16, f32 = jnp.bfloat16, jnp.float32
    return pl.pallas_call(
        kernel,
        out_shape=(pltpu.VMEM((ROWS, WIDTH), bf16), pltpu.VMEM((128, WIDTH), f32)),
        in_specs=[any_space] * 4 + [pl.BlockSpec(memory_space=pltpu.VMEM), smem, smem],
        out_specs=(pl.BlockSpec(memory_space=pltpu.VMEM),) * 2,
        scratch_shapes=[
            pltpu.VMEM((FSDP, ROWS, 512), bf16),
            pltpu.VMEM((D, WIDTH), bf16),
            pltpu.VMEM((TILES, ROWS, TILE), f32),
            pltpu.VMEM((BANK, 128), bf16),
            pltpu.VMEM((BANK, WIDTH), bf16),
            pltpu.VMEM((FACTORS, 128), f32),
            pltpu.VMEM((FACTORS, WIDTH), bf16),
            pltpu.VMEM((SLOT, WIDTH), bf16),
            pltpu.VMEM((PIECES, TILE, SLOT), bf16),
            pltpu.VMEM((POP, 16, 128), bf16),
            pltpu.VMEM((POP, 16, 128), bf16),
            pltpu.VMEM((ROWS, SLOT), f32),
            dma((64,)),
            dma((62,)),
            dma((16,)),
            dma((14,)),
            dma((POP,)),
            dma((POP,)),
            dma((4,)),
        ],
        compiler_params=pltpu.CompilerParams(
            collective_id=1, has_side_effects=True, vmem_limit_bytes=56 * 2**20
        ),
        name="gather_project",
    )(tokens, up_weight, a_bank, b_bank, factor_index.T, mirror, rewards)


def solution(mesh):
    in_specs = (
        P("pop", "fsdp"),
        P("pop", "fsdp"),
        P(None, "pop"),
        P(None, "fsdp"),
        P(),
        P("pop"),
        P("pop"),
    )
    out_specs = (P("pop", "fsdp"), P("pop", "fsdp"))
    return jax.shard_map(
        per_device, mesh=mesh, in_specs=in_specs, out_specs=out_specs, check_vma=False
    )
```

```python
import math

import jax
import jax.numpy as jnp
from jax import lax
from jax.experimental import pallas as pl
from jax.experimental.pallas import tpu as pltpu
from jax.sharding import PartitionSpec as P

D = 4096
RANK = 4
SEQ = 448
MEMBERS = 64
BANK = 1024
ROWS = 896
WIDTH = 1792
TILE = 256
TILES = WIDTH // TILE
PIECES = D // TILE
X, Z, CORES = 4, 8, 2
POP, FSDP = 32, 8
FACTORS = MEMBERS * RANK
SLOT = 128
LAST = 6

noise_scale = 0.5
MESH = pl.DeviceIdType.MESH


def picked(values, table):
    return jnp.dot(values.astype(jnp.bfloat16), table, preferred_element_type=jnp.float32)


def flat_rows(index, rows, first, period):
    row = lax.broadcasted_iota(jnp.int32, (rows, MEMBERS), 0)
    factor = first + lax.rem(row, period)
    chosen = lax.broadcasted_iota(jnp.int32, (rows, MEMBERS), 1) == lax.div(factor, RANK)
    whole = index[...]
    high = lax.div(whole, 32)
    low = whole - high * 32
    parts = [
        lax.dot_general(
            chosen.astype(jnp.bfloat16),
            part.astype(jnp.float32).astype(jnp.bfloat16),
            (((1,), (1,)), ((), ())),
            preferred_element_type=jnp.float32,
        )
        for part in (high, low)
    ]
    of_member = (parts[0] * 32.0 + parts[1]).astype(jnp.int32)
    row = lax.broadcasted_iota(jnp.int32, (rows, RANK), 0)
    rank = lax.rem(first + lax.rem(row, period), RANK)
    column = lax.broadcasted_iota(jnp.int32, (rows, RANK), 1)
    return jnp.sum(jnp.where(column == rank, of_member, 0), axis=1, keepdims=True)


def one_hot(rows_of, rows):
    return (lax.broadcasted_iota(jnp.int32, (rows, BANK), 1) == rows_of).astype(jnp.float32)


def kernel(
    tokens, weight, a_bank, b_bank, index, mirror, rewards,
    acc, low, own_b, update,
    tok, wts, banka, bankb, pick_a, pick_b, own_a, message, heard,
    w_got, w_sent, t_got, t_sent, m_got, m_sent, local,
):
    p = lax.axis_index("pop")
    f = lax.axis_index("fsdp")
    yl, z, c = p // 16, (p // 2) % Z, p % 2
    yh, x = f // X, f % X

    def pop_of(yl_, z_, c_):
        return yl_ * 16 + lax.rem(z_ + 2 * Z, Z) * 2 + c_

    def fsdp_of(yh_, x_):
        return yh_ * X + lax.rem(x_ + 2 * X, X)

    def sibling():
        return {"pop": pop_of(yl, z, 1 - c), "fsdp": f}

    def along_z(way):
        return {"pop": pop_of(yl, z + way, c), "fsdp": f}

    def across_y():
        return {"pop": pop_of(1 - yl, z, c), "fsdp": f}

    def along_x(way):
        return {"pop": p, "fsdp": fsdp_of(yh, x + way)}

    def far_y():
        return {"pop": p, "fsdp": fsdp_of(1 - yh, x)}

    barrier = pltpu.get_barrier_semaphore()

    def greet(j, _):
        peer = lax.rem(p + j, POP)
        pl.semaphore_signal(barrier, inc=1, device_id={"pop": peer, "fsdp": f}, device_id_type=MESH)
        return 0

    for way in (1, -1):
        pl.semaphore_signal(barrier, inc=1, device_id=along_x(way), device_id_type=MESH)
    pl.semaphore_signal(barrier, inc=1, device_id=far_y(), device_id_type=MESH)
    lax.fori_loop(1, POP, greet, 0)

    load_a = pltpu.make_async_copy(a_bank, banka, local.at[0])
    load_b = pltpu.make_async_copy(b_bank, bankb, local.at[1])
    load_t = pltpu.make_async_copy(tokens, tok.at[f], local.at[2])
    load_w = pltpu.make_async_copy(
        weight, wts.at[pl.ds(pl.multiple_of(p * 128, 128), 128)], local.at[3]
    )
    for copy in (load_a, load_w, load_t, load_b):
        copy.start()

    load_a.wait()
    hot = one_hot(flat_rows(index, FACTORS, 0, FACTORS), FACTORS).astype(jnp.bfloat16)
    rows_a = picked(hot, banka[...])
    pick_a[...] = rows_a
    line = lax.broadcasted_iota(jnp.int32, (8, 128), 0)
    info = jnp.where(
        line == 0,
        rewards[0].astype(jnp.float32),
        jnp.where(
            line == 1,
            rewards[1].astype(jnp.float32),
            jnp.where(line == 2, mirror[0].astype(jnp.float32), mirror[1].astype(jnp.float32)),
        ),
    )
    message[...] = jnp.concatenate(
        [rows_a.reshape(POP, 8, 128), jnp.broadcast_to(info[None], (POP, 8, 128))], axis=1
    ).astype(jnp.bfloat16)

    heard[p] = message[p]
    pl.semaphore_wait(barrier, POP - 1 + 3)

    sends = []

    def w_block(shard, half):
        return wts.at[pl.ds(pl.multiple_of(shard * 128 + half * 64, 64), 64)]

    def t_block(owner, half):
        return tok.at[owner, pl.ds(half * SEQ, SEQ)]

    counts = {"w": 0, "t": 0}

    def send_w(shard, half, target, own=False):
        k = counts["w"]
        counts["w"] += 1
        copy = pltpu.make_async_remote_copy(
            src_ref=weight.at[pl.ds(half * 64, 64)] if own else w_block(shard, half),
            dst_ref=w_block(shard, half),
            send_sem=w_sent.at[k],
            recv_sem=w_got.at[shard * 2 + half],
            device_id=target,
            device_id_type=MESH,
        )
        copy.start()
        sends.append(copy)

    def send_t(owner, half, target, own=False):
        k = counts["t"]
        counts["t"] += 1
        copy = pltpu.make_async_remote_copy(
            src_ref=tokens.at[pl.ds(half * SEQ, SEQ)] if own else t_block(owner, half),
            dst_ref=t_block(owner, half),
            send_sem=t_sent.at[k],
            recv_sem=t_got.at[owner * 2 + half],
            device_id=target,
            device_id_type=MESH,
        )
        copy.start()
        sends.append(copy)

    def wait_w(shard, half):
        block = w_block(shard, half)
        pltpu.make_async_copy(block, block, w_got.at[shard * 2 + half]).wait()

    def wait_t(owner, half):
        block = t_block(owner, half)
        pltpu.make_async_copy(block, block, t_got.at[owner * 2 + half]).wait()

    for turn in (0, 1):
        for way in (1, -1):
            send_w(p, turn if way == 1 else 1 - turn, along_z(way), True)
        for way in (1, -1):
            send_t(f, turn if way == 1 else 1 - turn, along_x(way), True)
        if turn == 0:
            def tell(j, _):
                peer = lax.rem(p + j, POP)
                pltpu.make_async_remote_copy(
                    src_ref=message.at[peer],
                    dst_ref=heard.at[p],
                    send_sem=m_sent.at[j],
                    recv_sem=m_got.at[p],
                    device_id={"pop": peer, "fsdp": f},
                    device_id_type=MESH,
                ).start()
                return 0

            lax.fori_loop(1, POP, tell, 0)
        send_t(f, turn, far_y(), True)
        send_w(p, turn, across_y(), True)
        send_w(p, turn, sibling(), True)

    def phase_of(q):
        x_, yl_, z_ = (q // 2) % X, q // Z, q % Z
        dx = lax.rem(x_ - x + X, X)
        dz = lax.rem(z_ - z + Z, Z)
        dz = jnp.minimum(dz, Z - dz)
        near = jnp.where(dx == 2, 2, 1)
        far = jnp.where(dx == 0, 2, jnp.where(dx == 2, 6, 4))
        by_tokens = jnp.where(yl_ == yh, near, far)
        same = jnp.where(dz < 3, 1, 2)
        other = jnp.where(
            dz == 0, 1, jnp.where(dz == 1, 3, jnp.where(dz == 2, 5, jnp.where(dz == 3, 6, 4)))
        )
        by_weight = jnp.where(yl_ == yl, same, other)
        return jnp.maximum(by_tokens, by_weight)


    keys = [phase_of(q) * PIECES + q for q in range(PIECES)]
    places = [sum((other < key).astype(jnp.int32) for other in keys if other is not key) for key in keys]
    ends = [
        sum((key < (number + 1) * PIECES).astype(jnp.int32) for key in keys)
        for number in range(LAST + 1)
    ]

    def piece_at(k):
        return sum(jnp.where(place == k, q, 0) for q, place in enumerate(places))

    owed = [(pop_of(yl, z, 1 - c), 0), (pop_of(yl, z, 1 - c), 1)]

    def settle():
        for shard, half in owed:
            wait_w(shard, half)
        owed.clear()

    def got_own(d, way, half):
        z_ = z - way * d
        shard = pop_of(yl, z_, c)
        wait_w(shard, half)
        if d < 3 or (d == 3 and half == (0 if way == 1 else 1)):
            send_w(shard, half, along_z(way))
        send_w(shard, half, sibling())
        if (d == 3 and half == 1) or d == 4:
            send_w(shard, half, across_y())
        owed.append((pop_of(yl, z_, 1 - c), half))

    def got_other(d, way, half, forward=True):
        z_ = z - way * d
        shard = pop_of(1 - yl, z_, c)
        wait_w(shard, half)
        if forward and (d == 1 or (d == 2 and half == 0)):
            send_w(shard, half, along_z(way))
        send_w(shard, half, sibling())
        owed.append((pop_of(1 - yl, z_, 1 - c), half))

    def pass_other(half):
        for way in (1, -1):
            send_w(pop_of(1 - yl, z, c), half, along_z(way))

    def got_tokens(yh_, d, way, half):
        owner = fsdp_of(yh_, x - way * d)
        wait_t(owner, half)
        if d == 1 and half == (0 if way == 1 else 1):
            send_t(owner, half, along_x(way))

    def pass_tokens(turn):
        for way in (1, -1):
            send_t(fsdp_of(1 - yh, x), turn if way == 1 else 1 - turn, along_x(way))

    def work(q):
        lhs = tok[lax.div(q, 2), :, pl.ds(pl.multiple_of(lax.rem(q, 2) * TILE, TILE), TILE)]
        features = pl.ds(pl.multiple_of(q * TILE, TILE), TILE)
        for n in range(TILES):
            acc[n] += jnp.dot(
                lhs, wts[features, n * TILE : (n + 1) * TILE], preferred_element_type=jnp.float32
            )
        low[...] += jnp.dot(lhs, own_a[q], preferred_element_type=jnp.float32)

    done = [0]

    def multiply(number, most):
        stop = jnp.minimum(done[0] + most, ends[number])

        def step(k, _):
            work(piece_at(k))
            return 0

        lax.fori_loop(done[0], stop, step, 0)
        done[0] = stop

    def own_turn(d, turn):
        for way in (1, -1):
            got_own(d, way, turn if way == 1 else 1 - turn)

    def other_turn(d, half, forward=True):
        for way in (1, -1):
            got_other(d, way, half, forward)

    def token_turn(yh_, turn):
        for way in (1, -1):
            got_tokens(yh_, 1, way, turn if way == 1 else 1 - turn)

    own_turn(1, 0)
    load_b.wait()
    pick_b[...] = picked(hot, bankb[...]).astype(jnp.bfloat16)
    own_turn(1, 1)
    token_turn(yh, 0)
    hot_own = one_hot(flat_rows(index, SLOT, p * 8, 8), SLOT)
    used = lax.broadcasted_iota(jnp.int32, (SLOT, BANK), 0) < 24
    own_b[...] = picked(jnp.where(used, hot_own, 0.0), bankb[...]).astype(jnp.bfloat16)
    own_turn(2, 0)
    acc[...] = jnp.zeros_like(acc)
    low[...] = jnp.zeros_like(low)
    load_t.wait()
    load_w.wait()
    own_turn(2, 1)
    token_turn(yh, 1)

    def hear(j, _):
        peer = lax.rem(p + POP - j, POP)
        block = heard.at[peer]
        pltpu.make_async_copy(block, block, m_got.at[peer]).wait()
        return 0

    lax.fori_loop(1, POP, hear, 0)

    def lay(q, _):
        both = jnp.concatenate([heard[2 * q], heard[2 * q + 1]], axis=1).astype(jnp.float32)[:8]
        own_a[q] = jnp.concatenate(
            [both, both, both, jnp.zeros((SLOT - 24, TILE), jnp.float32)], axis=0
        ).T.astype(jnp.bfloat16)
        return 0

    lax.fori_loop(0, PIECES, lay, 0)

    for half in (0, 1):
        got_other(0, 1, half)
    own_turn(3, 0)
    settle()
    multiply(1, 2)
    wait_t(fsdp_of(1 - yh, x), 0)
    wait_t(fsdp_of(1 - yh, x), 1)
    for turn in (0, 1):
        pass_tokens(turn)
    own_turn(3, 1)
    pass_other(0)
    pass_other(1)
    got_tokens(yh, 2, 1, 0)
    got_tokens(yh, 2, -1, 1)
    multiply(1, 3)
    got_own(4, 1, 0)
    got_own(4, -1, 1)
    told = heard[...].astype(jnp.float32)[:, 8:16, :].reshape(POP * 8, 128)
    row = lax.broadcasted_iota(jnp.int32, (FACTORS, POP * 8), 0)
    place = lax.broadcasted_iota(jnp.int32, (FACTORS, POP * 8), 1)
    member = lax.div(row, RANK)
    spot = lax.div(member, 2) * 8 + lax.rem(member, 2)
    told16 = told.astype(jnp.bfloat16)
    reward_of = picked((place == spot).astype(jnp.float32), told16)
    mirror_of = picked((place == spot + 2).astype(jnp.float32), told16)
    lane = lax.broadcasted_iota(jnp.int32, (POP * 8, 128), 1)
    at = lax.broadcasted_iota(jnp.int32, (POP * 8, 128), 0)
    mine = at == lax.div(lane, 2) * 8 + lax.rem(lane, 2)
    across = jnp.sum(jnp.where(mine, told, 0.0), axis=0, keepdims=True)
    lane = lax.broadcasted_iota(jnp.int32, (FACTORS, 128), 1)
    member = lax.div(lax.broadcasted_iota(jnp.int32, (FACTORS, 128), 0), RANK)
    ahead = (across < reward_of) | ((across == reward_of) & (lane < member))
    standing = jnp.sum(
        jnp.where(ahead & (lane < MEMBERS), 1.0, 0.0), axis=1, keepdims=True
    )
    coeff = (2.0 * standing - (MEMBERS - 1)) * (2.0 * mirror_of - 1.0)
    shaped = pick_a[...] * coeff
    high = shaped.astype(jnp.bfloat16)
    rest = (shaped - high.astype(jnp.float32)).astype(jnp.bfloat16)
    both = jnp.concatenate([high, rest], axis=0).astype(jnp.float32).T.astype(jnp.bfloat16)
    rows_b = pick_b[...]
    total = jnp.dot(
        both, jnp.concatenate([rows_b, rows_b], axis=0), preferred_element_type=jnp.float32
    )
    update[...] = total * (1.0 / ((MEMBERS - 1) * math.sqrt(MEMBERS * RANK)))

    settle()
    multiply(2, 2)
    other_turn(1, 0)
    token_turn(1 - yh, 0)
    multiply(2, 3)
    other_turn(1, 1)
    other_turn(3, 1, False)
    settle()
    multiply(3, 3)
    other_turn(2, 0)
    got_other(4, 1, 0)
    got_other(4, -1, 1)
    token_turn(1 - yh, 1)
    settle()
    multiply(4, 5)
    other_turn(2, 1)
    settle()
    multiply(5, PIECES)
    other_turn(3, 0, False)
    settle()
    got_tokens(1 - yh, 2, 1, 0)
    got_tokens(1 - yh, 2, -1, 1)
    multiply(LAST, PIECES)

    for copy in sends:
        copy.wait_send()

    def told_all(j, _):
        peer = lax.rem(p + j, POP)
        pltpu.make_async_copy(message.at[peer], message.at[peer], m_sent.at[j]).wait()
        return 0

    lax.fori_loop(1, POP, told_all, 0)


def finish(acc, low, own_b, shaped, mirror, hidden, update, out, done):
    save = pltpu.make_async_copy(shaped, update, done.at[TILES])
    save.start()
    lane = lax.broadcasted_iota(jnp.int32, (ROWS, SLOT), 1)
    row = lax.broadcasted_iota(jnp.int32, (ROWS, SLOT), 0)
    own = lax.div(lax.rem(lane, 8), RANK) == lax.div(row, SEQ)
    signed = jnp.where(
        row < SEQ,
        (2 * mirror[0] - 1).astype(jnp.float32),
        (2 * mirror[1] - 1).astype(jnp.float32),
    )
    scaled = jnp.where(own, low[...] * (signed * (noise_scale / math.sqrt(D * RANK))), 0.0)
    first = scaled.astype(jnp.bfloat16).astype(jnp.float32)
    second = (scaled - first).astype(jnp.bfloat16).astype(jnp.float32)
    third = scaled - first - second
    parts = jnp.where(lane < 8, first, jnp.where(lane < 16, second, third)).astype(jnp.bfloat16)

    saves = [save]
    for n in range(TILES):
        columns = pl.ds(n * TILE, TILE)
        out[:, columns] = (
            acc[n] + jnp.dot(parts, own_b[:, columns], preferred_element_type=jnp.float32)
        ).astype(jnp.bfloat16)
        saves.append(pltpu.make_async_copy(out.at[:, columns], hidden.at[:, columns], done.at[n]))
        saves[-1].start()
    for save in saves:
        save.wait()


def per_device(tokens, up_weight, a_bank, b_bank, factor_index, mirror, rewards):
    any_space = pl.BlockSpec(memory_space=pl.ANY)
    smem = pl.BlockSpec(memory_space=pltpu.SMEM)
    vmem = pl.BlockSpec(memory_space=pltpu.VMEM)
    dma = pltpu.SemaphoreType.DMA
    bf16, f32 = jnp.bfloat16, jnp.float32
    acc, low, own_b, shaped = pl.pallas_call(
        kernel,
        out_shape=(
            pltpu.VMEM((TILES, ROWS, TILE), f32),
            pltpu.VMEM((ROWS, SLOT), f32),
            pltpu.VMEM((SLOT, WIDTH), bf16),
            pltpu.VMEM((128, WIDTH), f32),
        ),
        in_specs=[any_space] * 4 + [vmem, smem, smem],
        out_specs=(vmem,) * 4,
        scratch_shapes=[
            pltpu.VMEM((FSDP, ROWS, 512), bf16),
            pltpu.VMEM((D, WIDTH), bf16),
            pltpu.VMEM((BANK, 128), bf16),
            pltpu.VMEM((BANK, WIDTH), bf16),
            pltpu.VMEM((FACTORS, 128), f32),
            pltpu.VMEM((FACTORS, WIDTH), bf16),
            pltpu.VMEM((PIECES, TILE, SLOT), bf16),
            pltpu.VMEM((POP, 16, 128), bf16),
            pltpu.VMEM((POP, 16, 128), bf16),
            dma((64,)),
            dma((62,)),
            dma((16,)),
            dma((14,)),
            dma((POP,)),
            dma((POP,)),
            dma((4,)),
        ],
        compiler_params=pltpu.CompilerParams(
            collective_id=1, has_side_effects=True, vmem_limit_bytes=55 * 2**20
        ),
        name="gather_project",
    )(tokens, up_weight, a_bank, b_bank, factor_index.T, mirror, rewards)
    held = [
        pltpu.with_memory_space_constraint(array, pltpu.VMEM)
        for array in (acc, low, own_b, shaped)
    ]
    return pl.pallas_call(
        finish,
        out_shape=(
            jax.ShapeDtypeStruct((ROWS, WIDTH), bf16),
            jax.ShapeDtypeStruct((128, WIDTH), f32),
        ),
        in_specs=[vmem] * 4 + [smem],
        out_specs=(any_space, any_space),
        scratch_shapes=[pltpu.VMEM((ROWS, WIDTH), bf16), dma((TILES + 1,))],
        compiler_params=pltpu.CompilerParams(vmem_limit_bytes=16 * 2**20),
        name="finish",
    )(*held, mirror)


def solution(mesh):
    in_specs = (
        P("pop", "fsdp"),
        P("pop", "fsdp"),
        P(None, "pop"),
        P(None, "fsdp"),
        P(),
        P("pop"),
        P("pop"),
    )
    out_specs = (P("pop", "fsdp"), P("pop", "fsdp"))
    return jax.shard_map(
        per_device, mesh=mesh, in_specs=in_specs, out_specs=out_specs, check_vma=False
    )
```

```python
import math

import jax
import jax.numpy as jnp
from jax import lax
from jax.experimental import pallas as pl
from jax.experimental.pallas import tpu as pltpu
from jax.sharding import PartitionSpec as P

D = 4096
RANK = 4
SEQ = 448
MEMBERS = 64
BANK = 1024
ROWS = 896
WIDTH = 1792
TILE = 256
TILES = WIDTH // TILE
PIECES = D // TILE
X, Z, CORES = 4, 8, 2
POP, FSDP = 32, 8
FACTORS = MEMBERS * RANK
SLOT = 128
LAST = 6

noise_scale = 0.5
MESH = pl.DeviceIdType.MESH


def picked(values, table):
    return jnp.dot(values.astype(jnp.bfloat16), table, preferred_element_type=jnp.float32)


def flat_rows(index, rows, first, period):
    row = lax.broadcasted_iota(jnp.int32, (rows, MEMBERS), 0)
    factor = first + lax.rem(row, period)
    chosen = lax.broadcasted_iota(jnp.int32, (rows, MEMBERS), 1) == lax.div(factor, RANK)
    whole = index[...]
    high = lax.div(whole, 32)
    low = whole - high * 32
    parts = [
        lax.dot_general(
            chosen.astype(jnp.bfloat16),
            part.astype(jnp.float32).astype(jnp.bfloat16),
            (((1,), (1,)), ((), ())),
            preferred_element_type=jnp.float32,
        )
        for part in (high, low)
    ]
    of_member = (parts[0] * 32.0 + parts[1]).astype(jnp.int32)
    row = lax.broadcasted_iota(jnp.int32, (rows, RANK), 0)
    rank = lax.rem(first + lax.rem(row, period), RANK)
    column = lax.broadcasted_iota(jnp.int32, (rows, RANK), 1)
    return jnp.sum(jnp.where(column == rank, of_member, 0), axis=1, keepdims=True)


def one_hot(rows_of, rows):
    return (lax.broadcasted_iota(jnp.int32, (rows, BANK), 1) == rows_of).astype(jnp.float32)


def kernel(
    tokens, weight, a_bank, b_bank, index, mirror, rewards,
    acc, low, own_b, update,
    tok, wts, banka, bankb, pick_a, pick_b, own_a, message, heard,
    w_got, w_sent, t_got, t_sent, m_got, m_sent, local,
):
    p = lax.axis_index("pop")
    f = lax.axis_index("fsdp")
    yl, z, c = p // 16, (p // 2) % Z, p % 2
    yh, x = f // X, f % X

    def pop_of(yl_, z_, c_):
        return yl_ * 16 + lax.rem(z_ + 2 * Z, Z) * 2 + c_

    def fsdp_of(yh_, x_):
        return yh_ * X + lax.rem(x_ + 2 * X, X)

    def sibling():
        return {"pop": pop_of(yl, z, 1 - c), "fsdp": f}

    def along_z(way):
        return {"pop": pop_of(yl, z + way, c), "fsdp": f}

    def across_y():
        return {"pop": pop_of(1 - yl, z, c), "fsdp": f}

    def along_x(way):
        return {"pop": p, "fsdp": fsdp_of(yh, x + way)}

    def far_y():
        return {"pop": p, "fsdp": fsdp_of(1 - yh, x)}

    barrier = pltpu.get_barrier_semaphore()

    def greet(j, _):
        peer = lax.rem(p + j, POP)
        pl.semaphore_signal(barrier, inc=1, device_id={"pop": peer, "fsdp": f}, device_id_type=MESH)
        return 0

    for way in (1, -1):
        pl.semaphore_signal(barrier, inc=1, device_id=along_x(way), device_id_type=MESH)
    pl.semaphore_signal(barrier, inc=1, device_id=far_y(), device_id_type=MESH)
    lax.fori_loop(1, POP, greet, 0)

    load_a = pltpu.make_async_copy(a_bank, banka, local.at[0])
    load_b = pltpu.make_async_copy(b_bank, bankb, local.at[1])
    load_t = pltpu.make_async_copy(tokens, tok.at[f], local.at[2])
    load_w = pltpu.make_async_copy(
        weight, wts.at[pl.ds(pl.multiple_of(p * 128, 128), 128)], local.at[3]
    )
    for copy in (load_a, load_w, load_t, load_b):
        copy.start()

    load_a.wait()
    hot = one_hot(flat_rows(index, FACTORS, 0, FACTORS), FACTORS).astype(jnp.bfloat16)
    rows_a = picked(hot, banka[...])
    pick_a[...] = rows_a
    line = lax.broadcasted_iota(jnp.int32, (8, 128), 0)
    info = jnp.where(
        line == 0,
        rewards[0].astype(jnp.float32),
        jnp.where(
            line == 1,
            rewards[1].astype(jnp.float32),
            jnp.where(line == 2, mirror[0].astype(jnp.float32), mirror[1].astype(jnp.float32)),
        ),
    )
    message[...] = jnp.concatenate(
        [rows_a.reshape(POP, 8, 128), jnp.broadcast_to(info[None], (POP, 8, 128))], axis=1
    ).astype(jnp.bfloat16)

    heard[p] = message[p]
    pl.semaphore_wait(barrier, POP - 1 + 3)

    sends = []

    def w_block(shard, half):
        return wts.at[pl.ds(pl.multiple_of(shard * 128 + half * 64, 64), 64)]

    def t_block(owner, half):
        return tok.at[owner, pl.ds(half * SEQ, SEQ)]

    counts = {"w": 0, "t": 0}

    def send_w(shard, half, target, own=False):
        k = counts["w"]
        counts["w"] += 1
        copy = pltpu.make_async_remote_copy(
            src_ref=weight.at[pl.ds(half * 64, 64)] if own else w_block(shard, half),
            dst_ref=w_block(shard, half),
            send_sem=w_sent.at[k],
            recv_sem=w_got.at[shard * 2 + half],
            device_id=target,
            device_id_type=MESH,
        )
        copy.start()
        sends.append(copy)

    def send_t(owner, half, target, own=False):
        k = counts["t"]
        counts["t"] += 1
        copy = pltpu.make_async_remote_copy(
            src_ref=tokens.at[pl.ds(half * SEQ, SEQ)] if own else t_block(owner, half),
            dst_ref=t_block(owner, half),
            send_sem=t_sent.at[k],
            recv_sem=t_got.at[owner * 2 + half],
            device_id=target,
            device_id_type=MESH,
        )
        copy.start()
        sends.append(copy)

    def wait_w(shard, half):
        block = w_block(shard, half)
        pltpu.make_async_copy(block, block, w_got.at[shard * 2 + half]).wait()

    def wait_t(owner, half):
        block = t_block(owner, half)
        pltpu.make_async_copy(block, block, t_got.at[owner * 2 + half]).wait()

    for turn in (0, 1):
        for way in (1, -1):
            send_w(p, turn if way == 1 else 1 - turn, along_z(way), True)
        for way in (1, -1):
            send_t(f, turn if way == 1 else 1 - turn, along_x(way), True)
        if turn == 0:
            def tell(j, _):
                peer = lax.rem(p + j, POP)
                pltpu.make_async_remote_copy(
                    src_ref=message.at[peer],
                    dst_ref=heard.at[p],
                    send_sem=m_sent.at[j],
                    recv_sem=m_got.at[p],
                    device_id={"pop": peer, "fsdp": f},
                    device_id_type=MESH,
                ).start()
                return 0

            lax.fori_loop(1, POP, tell, 0)
        send_t(f, turn, far_y(), True)
        send_w(p, turn, across_y(), True)
        send_w(p, turn, sibling(), True)

    def phase_of(q):
        x_, yl_, z_ = (q // 2) % X, q // Z, q % Z
        dx = lax.rem(x_ - x + X, X)
        dz = lax.rem(z_ - z + Z, Z)
        dz = jnp.minimum(dz, Z - dz)
        near = jnp.where(dx == 2, 2, 1)
        far = jnp.where(dx == 0, 2, jnp.where(dx == 2, 6, 4))
        by_tokens = jnp.where(yl_ == yh, near, far)
        same = jnp.where(dz < 3, 1, 2)
        other = jnp.where(
            dz == 0, 1, jnp.where(dz == 1, 3, jnp.where(dz == 2, 5, jnp.where(dz == 3, 6, 4)))
        )
        by_weight = jnp.where(yl_ == yl, same, other)
        return jnp.maximum(by_tokens, by_weight)


    keys = [phase_of(q) * PIECES + q for q in range(PIECES)]
    places = [sum((other < key).astype(jnp.int32) for other in keys if other is not key) for key in keys]
    ends = [
        sum((key < (number + 1) * PIECES).astype(jnp.int32) for key in keys)
        for number in range(LAST + 1)
    ]

    def piece_at(k):
        return sum(jnp.where(place == k, q, 0) for q, place in enumerate(places))

    owed = [(pop_of(yl, z, 1 - c), 0), (pop_of(yl, z, 1 - c), 1)]

    def settle():
        for shard, half in owed:
            wait_w(shard, half)
        owed.clear()

    def got_own(d, way, half):
        z_ = z - way * d
        shard = pop_of(yl, z_, c)
        wait_w(shard, half)
        if d < 3 or (d == 3 and half == (0 if way == 1 else 1)):
            send_w(shard, half, along_z(way))
        send_w(shard, half, sibling())
        if (d == 3 and half == 1) or d == 4:
            send_w(shard, half, across_y())
        owed.append((pop_of(yl, z_, 1 - c), half))

    def got_other(d, way, half, forward=True):
        z_ = z - way * d
        shard = pop_of(1 - yl, z_, c)
        wait_w(shard, half)
        if forward and (d == 1 or (d == 2 and half == 0)):
            send_w(shard, half, along_z(way))
        send_w(shard, half, sibling())
        owed.append((pop_of(1 - yl, z_, 1 - c), half))

    def pass_other(half):
        for way in (1, -1):
            send_w(pop_of(1 - yl, z, c), half, along_z(way))

    def got_tokens(yh_, d, way, half):
        owner = fsdp_of(yh_, x - way * d)
        wait_t(owner, half)
        if d == 1 and half == (0 if way == 1 else 1):
            send_t(owner, half, along_x(way))

    def pass_tokens(turn):
        for way in (1, -1):
            send_t(fsdp_of(1 - yh, x), turn if way == 1 else 1 - turn, along_x(way))

    def work(q):
        lhs = tok[lax.div(q, 2), :, pl.ds(pl.multiple_of(lax.rem(q, 2) * TILE, TILE), TILE)]
        features = pl.ds(pl.multiple_of(q * TILE, TILE), TILE)
        for n in range(TILES):
            acc[n] += jnp.dot(
                lhs, wts[features, n * TILE : (n + 1) * TILE], preferred_element_type=jnp.float32
            )
        low[...] += jnp.dot(lhs, own_a[q], preferred_element_type=jnp.float32)

    done = [0]

    def multiply(number, most):
        stop = jnp.minimum(done[0] + most, ends[number])

        def step(k, _):
            work(piece_at(k))
            return 0

        lax.fori_loop(done[0], stop, step, 0)
        done[0] = stop

    def own_turn(d, turn):
        for way in (1, -1):
            got_own(d, way, turn if way == 1 else 1 - turn)

    def other_turn(d, half, forward=True):
        for way in (1, -1):
            got_other(d, way, half, forward)

    def token_turn(yh_, turn):
        for way in (1, -1):
            got_tokens(yh_, 1, way, turn if way == 1 else 1 - turn)

    own_turn(1, 0)
    load_b.wait()
    pick_b[...] = picked(hot, bankb[...]).astype(jnp.bfloat16)
    own_turn(1, 1)
    token_turn(yh, 0)
    hot_own = one_hot(flat_rows(index, SLOT, p * 8, 8), SLOT)
    used = lax.broadcasted_iota(jnp.int32, (SLOT, BANK), 0) < 24
    own_b[...] = picked(jnp.where(used, hot_own, 0.0), bankb[...]).astype(jnp.bfloat16)
    own_turn(2, 0)
    acc[...] = jnp.zeros_like(acc)
    low[...] = jnp.zeros_like(low)
    load_t.wait()
    load_w.wait()
    own_turn(2, 1)
    token_turn(yh, 1)

    def hear(j, _):
        peer = lax.rem(p + POP - j, POP)
        block = heard.at[peer]
        pltpu.make_async_copy(block, block, m_got.at[peer]).wait()
        return 0

    lax.fori_loop(1, POP, hear, 0)

    def lay(q, _):
        both = jnp.concatenate([heard[2 * q], heard[2 * q + 1]], axis=1).astype(jnp.float32)[:8]
        own_a[q] = jnp.concatenate(
            [both, both, both, jnp.zeros((SLOT - 24, TILE), jnp.float32)], axis=0
        ).T.astype(jnp.bfloat16)
        return 0

    lax.fori_loop(0, PIECES, lay, 0)

    for half in (0, 1):
        got_other(0, 1, half)
    own_turn(3, 0)
    settle()
    multiply(1, 2)
    wait_t(fsdp_of(1 - yh, x), 0)
    wait_t(fsdp_of(1 - yh, x), 1)
    for turn in (0, 1):
        pass_tokens(turn)
    own_turn(3, 1)
    pass_other(0)
    pass_other(1)
    got_tokens(yh, 2, 1, 0)
    got_tokens(yh, 2, -1, 1)
    multiply(1, 3)
    got_own(4, 1, 0)
    got_own(4, -1, 1)
    told = heard[...].astype(jnp.float32)[:, 8:16, :].reshape(POP * 8, 128)
    row = lax.broadcasted_iota(jnp.int32, (FACTORS, POP * 8), 0)
    place = lax.broadcasted_iota(jnp.int32, (FACTORS, POP * 8), 1)
    member = lax.div(row, RANK)
    spot = lax.div(member, 2) * 8 + lax.rem(member, 2)
    told16 = told.astype(jnp.bfloat16)
    reward_of = picked((place == spot).astype(jnp.float32), told16)
    mirror_of = picked((place == spot + 2).astype(jnp.float32), told16)
    lane = lax.broadcasted_iota(jnp.int32, (POP * 8, 128), 1)
    at = lax.broadcasted_iota(jnp.int32, (POP * 8, 128), 0)
    mine = at == lax.div(lane, 2) * 8 + lax.rem(lane, 2)
    across = jnp.sum(jnp.where(mine, told, 0.0), axis=0, keepdims=True)
    lane = lax.broadcasted_iota(jnp.int32, (FACTORS, 128), 1)
    member = lax.div(lax.broadcasted_iota(jnp.int32, (FACTORS, 128), 0), RANK)
    ahead = (across < reward_of) | ((across == reward_of) & (lane < member))
    standing = jnp.sum(
        jnp.where(ahead & (lane < MEMBERS), 1.0, 0.0), axis=1, keepdims=True
    )
    coeff = (2.0 * standing - (MEMBERS - 1)) * (2.0 * mirror_of - 1.0)
    shaped = pick_a[...] * coeff
    high = shaped.astype(jnp.bfloat16)
    rest = (shaped - high.astype(jnp.float32)).astype(jnp.bfloat16)
    both = jnp.concatenate([high, rest], axis=0).astype(jnp.float32).T.astype(jnp.bfloat16)
    rows_b = pick_b[...]
    total = jnp.dot(
        both, jnp.concatenate([rows_b, rows_b], axis=0), preferred_element_type=jnp.float32
    )
    update[...] = total * (1.0 / ((MEMBERS - 1) * math.sqrt(MEMBERS * RANK)))

    settle()
    multiply(2, 2)
    other_turn(1, 0)
    token_turn(1 - yh, 0)
    multiply(2, 3)
    other_turn(1, 1)
    other_turn(3, 1, False)
    settle()
    multiply(3, 3)
    other_turn(2, 0)
    got_other(4, 1, 0)
    got_other(4, -1, 1)
    token_turn(1 - yh, 1)
    settle()
    multiply(4, 5)
    other_turn(2, 1)
    settle()
    multiply(5, 3)
    other_turn(3, 0, False)
    multiply(5, PIECES)
    settle()
    got_tokens(1 - yh, 2, 1, 0)
    got_tokens(1 - yh, 2, -1, 1)
    multiply(LAST, PIECES)

    for copy in sends:
        copy.wait_send()

    def told_all(j, _):
        peer = lax.rem(p + j, POP)
        pltpu.make_async_copy(message.at[peer], message.at[peer], m_sent.at[j]).wait()
        return 0

    lax.fori_loop(1, POP, told_all, 0)


def finish(acc, low, own_b, shaped, mirror, hidden, update, out, done):
    save = pltpu.make_async_copy(shaped, update, done.at[TILES])
    save.start()
    lane = lax.broadcasted_iota(jnp.int32, (ROWS, SLOT), 1)
    row = lax.broadcasted_iota(jnp.int32, (ROWS, SLOT), 0)
    own = lax.div(lax.rem(lane, 8), RANK) == lax.div(row, SEQ)
    signed = jnp.where(
        row < SEQ,
        (2 * mirror[0] - 1).astype(jnp.float32),
        (2 * mirror[1] - 1).astype(jnp.float32),
    )
    scaled = jnp.where(own, low[...] * (signed * (noise_scale / math.sqrt(D * RANK))), 0.0)
    first = scaled.astype(jnp.bfloat16).astype(jnp.float32)
    second = (scaled - first).astype(jnp.bfloat16).astype(jnp.float32)
    third = scaled - first - second
    parts = jnp.where(lane < 8, first, jnp.where(lane < 16, second, third)).astype(jnp.bfloat16)

    saves = [save]
    for n in range(TILES):
        columns = pl.ds(n * TILE, TILE)
        out[:, columns] = (
            acc[n] + jnp.dot(parts, own_b[:, columns], preferred_element_type=jnp.float32)
        ).astype(jnp.bfloat16)
        saves.append(pltpu.make_async_copy(out.at[:, columns], hidden.at[:, columns], done.at[n]))
        saves[-1].start()
    for save in saves:
        save.wait()


def per_device(tokens, up_weight, a_bank, b_bank, factor_index, mirror, rewards):
    any_space = pl.BlockSpec(memory_space=pl.ANY)
    smem = pl.BlockSpec(memory_space=pltpu.SMEM)
    vmem = pl.BlockSpec(memory_space=pltpu.VMEM)
    dma = pltpu.SemaphoreType.DMA
    bf16, f32 = jnp.bfloat16, jnp.float32
    acc, low, own_b, shaped = pl.pallas_call(
        kernel,
        out_shape=(
            pltpu.VMEM((TILES, ROWS, TILE), f32),
            pltpu.VMEM((ROWS, SLOT), f32),
            pltpu.VMEM((SLOT, WIDTH), bf16),
            pltpu.VMEM((128, WIDTH), f32),
        ),
        in_specs=[any_space] * 4 + [vmem, smem, smem],
        out_specs=(vmem,) * 4,
        scratch_shapes=[
            pltpu.VMEM((FSDP, ROWS, 512), bf16),
            pltpu.VMEM((D, WIDTH), bf16),
            pltpu.VMEM((BANK, 128), bf16),
            pltpu.VMEM((BANK, WIDTH), bf16),
            pltpu.VMEM((FACTORS, 128), f32),
            pltpu.VMEM((FACTORS, WIDTH), bf16),
            pltpu.VMEM((PIECES, TILE, SLOT), bf16),
            pltpu.VMEM((POP, 16, 128), bf16),
            pltpu.VMEM((POP, 16, 128), bf16),
            dma((64,)),
            dma((62,)),
            dma((16,)),
            dma((14,)),
            dma((POP,)),
            dma((POP,)),
            dma((4,)),
        ],
        compiler_params=pltpu.CompilerParams(
            collective_id=1, has_side_effects=True, vmem_limit_bytes=55 * 2**20
        ),
        name="gather_project",
    )(tokens, up_weight, a_bank, b_bank, factor_index.T, mirror, rewards)
    held = [
        pltpu.with_memory_space_constraint(array, pltpu.VMEM)
        for array in (acc, low, own_b, shaped)
    ]
    return pl.pallas_call(
        finish,
        out_shape=(
            jax.ShapeDtypeStruct((ROWS, WIDTH), bf16),
            jax.ShapeDtypeStruct((128, WIDTH), f32),
        ),
        in_specs=[vmem] * 4 + [smem],
        out_specs=(any_space, any_space),
        scratch_shapes=[pltpu.VMEM((ROWS, WIDTH), bf16), dma((TILES + 1,))],
        compiler_params=pltpu.CompilerParams(vmem_limit_bytes=16 * 2**20),
        name="finish",
    )(*held, mirror)


def solution(mesh):
    in_specs = (
        P("pop", "fsdp"),
        P("pop", "fsdp"),
        P(None, "pop"),
        P(None, "fsdp"),
        P(),
        P("pop"),
        P("pop"),
    )
    out_specs = (P("pop", "fsdp"), P("pop", "fsdp"))
    return jax.shard_map(
        per_device, mesh=mesh, in_specs=in_specs, out_specs=out_specs, check_vma=False
    )
```
